32 devices in a mesh: fsdp: 4 (over y, core), replica: 8 (over z, x).
Axes of the slice: x: 2, y: 2, z: 4, core: 2. Of those that a mesh axis runs over, the one named last changes fastest.
Arguments:
- tokens: bfloat16 [16384, 1024], P(('fsdp', 'replica')), may hold values from -6 to 6
- seq_lengths: int32 [32, 4], P(('fsdp', 'replica')), may hold values from 0 to 512, as said below
- attention_gain: bfloat16 [1024], P('fsdp'), may hold values from 0.5 to 1.5
- query_weight: bfloat16 [1024, 2048], P('fsdp'), may hold values from -0.1875 to 0.1875
- key_matrix: bfloat16 [1024, 1024], P('fsdp'), may hold values from -0.1875 to 0.1875
- value_matrix: bfloat16 [1024, 1024], P('fsdp'), may hold values from -0.1875 to 0.1875
- query_norm_gain: bfloat16 [128], P('fsdp'), may hold values from 0.5 to 1.5
- key_gain: bfloat16 [128], P('fsdp'), may hold values from 0.5 to 1.5
- out_weight: bfloat16 [2048, 1024], P('fsdp'), may hold values from -1 to 1
- feed_gain: bfloat16 [1024], P('fsdp'), may hold values from 0.5 to 1.5
- gate_weight: bfloat16 [1024, 3072], P('fsdp'), may hold values from -0.1875 to 0.1875
- up_weight: bfloat16 [1024, 3072], P('fsdp'), may hold values from -0.1875 to 0.1875
- down_weight: bfloat16 [3072, 1024], P('fsdp'), may hold values from -0.109375 to 0.109375
- cotangent: bfloat16 [16384, 1024], P(('fsdp', 'replica')), may hold values from -6 to 6
Outputs:
- output: bfloat16 [16384, 1024], P(('fsdp', 'replica'))
- grad_tokens: bfloat16 [16384, 1024], P(('fsdp', 'replica'))
- grad_attention_gain: float32 [1024], P('fsdp')
- grad_query_weight: float32 [1024, 2048], P('fsdp')
- grad_key_weight: float32 [1024, 1024], P('fsdp')
- grad_value_weight: float32 [1024, 1024], P('fsdp')
- grad_query_gain: float32 [128], P('fsdp')
- grad_key_gain: float32 [128], P('fsdp')
- grad_out_weight: float32 [2048, 1024], P('fsdp')
- grad_feed_gain: float32 [1024], P('fsdp')
- grad_gate_weight: float32 [1024, 3072], P('fsdp')
- grad_up_weight: float32 [1024, 3072], P('fsdp')
- grad_down_weight: float32 [3072, 1024], P('fsdp')
The draws below stay inside these ranges and needn't reach their ends.
Inputs may be any that keep to these rules, and one draw needn't show every extreme that they name: `seq_lengths`: row b lists the lengths of up to 4 sequences of the device whose buffer is b; the first entry is at least 1, unused slots are 0 and stand only after used ones. Each sequence fills ceil(length / 128) blocks of 128 slots, one after another from slot 0, and a row's sequences fill at most 4 blocks. Some row holds a single sequence of 512 tokens.
All inputs are finite; a program needn't handle non-finite values.
Results may differ from the reference program's by a relative error of at most 0.015.
Values may be sent and summed in bfloat16 or wider, within the bound.
A program may use at most 256 MiB of HBM per device.

```python
import math
import jax
import jax.numpy as jnp
from jax import lax

MODEL_WIDTH = 1024
QUERY_HEADS = 16
KEY_VALUE_HEADS = 8
HEAD_SIZE = 128
FF = 3072
BLOCK = 128
BLK_DEV = 4
SEQS_DEV = 4
TOK_DEV = 512
TOKENS = 16384
N_FSDP = 4
N_REPLICA = 8


def draw_seq_lengths(key, part):
    key = jax.random.fold_in(key, 7)
    rows = N_FSDP * N_REPLICA
    key_blocks, key_cap, key_tail, key_pick = jax.random.split(key, 4)
    most = min(8, BLK_DEV)
    blocks = jax.random.randint(key_blocks, (rows, SEQS_DEV), 1, most + 1)
    cap = jax.random.randint(key_cap, (rows, 1), BLK_DEV // 2, BLK_DEV + 1)
    ends = jnp.cumsum(blocks, axis=1)
    kept = jnp.where(ends <= cap, blocks, 0)
    kept = jnp.concatenate([jnp.minimum(blocks[:, :1], cap), kept[:, 1:]], axis=1)
    tail = jax.random.randint(key_tail, (rows, SEQS_DEV), 1, BLOCK + 1)
    lengths = jnp.where(kept > 0, BLOCK * (kept - 1) + tail, 0)
    longest = jnp.zeros((SEQS_DEV,), jnp.int32).at[0].set(most * BLOCK)
    chosen = jax.random.randint(key_pick, (), 0, rows)
    picked = (jnp.arange(rows) == chosen)[:, None]
    return jnp.where(picked, longest[None, :], lengths).astype(jnp.int32)


def levels(key, shape, pieces, least, largest):
    level = 1.0
    for axis_at, parts in pieces:
        steps = jax.random.uniform(jax.random.fold_in(jax.random.fold_in(key, 6), axis_at), (parts,), jnp.float32, least / len(pieces), largest / len(pieces))
        level = level * jnp.repeat(jnp.exp(steps), shape[axis_at] // parts).reshape((-1,) + (1,) * (len(shape) - 1 - axis_at))
    return level


def centred(rng, dims, width, reach, pieces=(), kind=jnp.bfloat16):
    level = levels(rng, dims, pieces, -0.22, 0.18) if pieces else 1.0
    drawn = jax.random.normal(rng, dims, jnp.float32) * width * level
    return jnp.minimum(jnp.maximum(drawn, -reach), reach).astype(kind)


def setup_inputs(seed: int = 0) -> dict:
    arg_keys = jax.random.split(jax.random.key(seed), 15)
    return {
        "tokens": centred(arg_keys[0], (TOKENS, MODEL_WIDTH), 1.0, 6.0, ((0, 32),)),
        "seq_lengths": draw_seq_lengths(jax.random.fold_in(arg_keys[14], 71), 0),
        "attention_gain": jnp.clip(1.0 + 0.1 * jax.random.normal(arg_keys[2], (MODEL_WIDTH,), jnp.float32), 0.5, 1.5).astype(jnp.bfloat16),
        "query_weight": centred(arg_keys[3], (MODEL_WIDTH, QUERY_HEADS * HEAD_SIZE), MODEL_WIDTH ** -0.5, 0.1875, ((0, 4),)),
        "key_matrix": centred(arg_keys[4], (MODEL_WIDTH, KEY_VALUE_HEADS * HEAD_SIZE), MODEL_WIDTH ** -0.5, 0.1875, ((0, 4),)),
        "value_matrix": centred(arg_keys[5], (MODEL_WIDTH, KEY_VALUE_HEADS * HEAD_SIZE), MODEL_WIDTH ** -0.5, 0.1875, ((0, 4),)),
        "query_norm_gain": jnp.clip(1.0 + 0.1 * jax.random.normal(arg_keys[6], (HEAD_SIZE,), jnp.float32), 0.5, 1.5).astype(jnp.bfloat16),
        "key_gain": jnp.clip(1.0 + 0.1 * jax.random.normal(arg_keys[7], (HEAD_SIZE,), jnp.float32), 0.5, 1.5).astype(jnp.bfloat16),
        "out_weight": centred(arg_keys[8], (QUERY_HEADS * HEAD_SIZE, MODEL_WIDTH), (max(QUERY_HEADS * HEAD_SIZE // 64, 1)) ** -0.5, 1.0, ((0, 4),)),
        "feed_gain": jnp.clip(1.0 + 0.1 * jax.random.normal(arg_keys[9], (MODEL_WIDTH,), jnp.float32), 0.5, 1.5).astype(jnp.bfloat16),
        "gate_weight": centred(arg_keys[10], (MODEL_WIDTH, FF), MODEL_WIDTH ** -0.5, 0.1875, ((0, 4),)),
        "up_weight": centred(arg_keys[11], (MODEL_WIDTH, FF), MODEL_WIDTH ** -0.5, 0.1875, ((0, 4),)),
        "down_weight": centred(arg_keys[12], (FF, MODEL_WIDTH), FF ** -0.5, 0.109375, ((0, 4),)),
        "cotangent": centred(arg_keys[13], (TOKENS, MODEL_WIDTH), 1.0, 6.0, ((0, 32),)),
    }


@jax.custom_vjp
def reduced_precision(v):
    return lax.optimization_barrier(v.astype(jnp.bfloat16)).astype(jnp.float32)

@jax.custom_vjp
def reduced_precision_backward(v):
    return v

def low_keep(v):
    return (reduced_precision(v), None)

def low_pass(kept, grad):
    return (grad,)

def back_keep(v):
    return (v, None)

def back_low(kept, grad):
    return (reduced_precision(grad),)
reduced_precision.defvjp(low_keep, low_pass)
reduced_precision_backward.defvjp(back_keep, back_low)
norm_eps = 1e-06
rope_base = 1000000.0

def matrix_product(left, right):
    return jnp.dot(left, right, precision=lax.Precision.HIGHEST, preferred_element_type=jnp.float32)

def root_mean_scale(value_rows, gain):
    return value_rows * lax.rsqrt(lax.optimization_barrier(jnp.mean(value_rows * value_rows, axis=-1, keepdims=True)) + norm_eps) * gain

def layout(lengths_row, token_count):
    blocks = ((lengths_row + BLOCK - 1) // BLOCK).astype(jnp.int32)
    ends = (jnp.cumsum(blocks) * BLOCK).astype(jnp.int32)
    starts = (ends - blocks * BLOCK).astype(jnp.int32)
    places = jnp.arange(token_count, dtype=jnp.int32)
    inside = (places[:, None] >= starts[None, :]) & (places[:, None] < starts[None, :] + lengths_row[None, :])
    numbers = jnp.arange(lengths_row.shape[0], dtype=jnp.int32) + 1
    segment = lax.optimization_barrier(jnp.sum(jnp.where(inside, numbers[None, :], 0), axis=1)).astype(jnp.int32)
    position = lax.optimization_barrier(jnp.sum(jnp.where(inside, places[:, None] - starts[None, :], 0), axis=1)).astype(jnp.int32)
    return (segment, position)

def rope_tables(position):
    half = HEAD_SIZE // 2
    freq = jnp.exp(-math.log(rope_base) * 2.0 * jnp.arange(half, dtype=jnp.float32) / HEAD_SIZE)
    angle = position.astype(jnp.float32)[:, None] * freq[None, :]
    return (jnp.cos(angle)[:, None, :], jnp.sin(angle)[:, None, :])

def apply_rotary(value_rows, cosine_table, sine_table):
    half = HEAD_SIZE // 2
    first_half = value_rows[..., :half]
    second_half = value_rows[..., half:]
    return jnp.concatenate([first_half * cosine_table - second_half * sine_table, second_half * cosine_table + first_half * sine_table], axis=-1)

def layer(inputs, segment, position, weights):
    attention_gain, query_weight, key_matrix, value_matrix, query_norm_gain, key_gain, out_weight, feed_gain, gate_weight, up_weight, down_weight = weights
    token_count = inputs.shape[0]
    head_groups = QUERY_HEADS // KEY_VALUE_HEADS
    hidden_state = reduced_precision(root_mean_scale(inputs, attention_gain))
    query_rows = reduced_precision_backward(matrix_product(hidden_state, query_weight)).reshape(token_count, QUERY_HEADS, HEAD_SIZE)
    key_rows = reduced_precision_backward(matrix_product(hidden_state, key_matrix)).reshape(token_count, KEY_VALUE_HEADS, HEAD_SIZE)
    value_rows = reduced_precision(reduced_precision_backward(matrix_product(hidden_state, value_matrix))).reshape(token_count, KEY_VALUE_HEADS, HEAD_SIZE)
    cosine_table, sine_table = rope_tables(position)
    query_rows = reduced_precision(apply_rotary(root_mean_scale(query_rows, query_norm_gain), cosine_table, sine_table)).reshape(token_count, KEY_VALUE_HEADS, head_groups, HEAD_SIZE)
    key_rows = reduced_precision(apply_rotary(root_mean_scale(key_rows, key_gain), cosine_table, sine_table))
    scores = reduced_precision_backward(jnp.einsum('qgrd,kgd->grqk', query_rows, key_rows, precision=lax.Precision.HIGHEST) / math.sqrt(HEAD_SIZE))
    places = jnp.arange(token_count, dtype=jnp.int32)
    allowed = (segment[:, None] == segment[None, :]) & (places[None, :] <= places[:, None])
    scores = jnp.where(allowed[None, None], scores, -1e+30)
    top = lax.optimization_barrier(jnp.max(scores, axis=-1, keepdims=True))
    weight = jnp.exp(scores - top)
    probs = reduced_precision(weight / lax.optimization_barrier(jnp.sum(weight, axis=-1, keepdims=True)))
    mixed = jnp.einsum('grqk,kgd->qgrd', probs, value_rows, precision=lax.Precision.HIGHEST)
    mixed = reduced_precision(reduced_precision_backward(mixed)).reshape(token_count, QUERY_HEADS * HEAD_SIZE)
    middle = inputs + reduced_precision_backward(matrix_product(mixed, out_weight))
    hidden2 = reduced_precision(root_mean_scale(middle, feed_gain))
    gate = reduced_precision_backward(matrix_product(hidden2, gate_weight))
    up = reduced_precision_backward(matrix_product(hidden2, up_weight))
    activation = reduced_precision(jax.nn.silu(gate) * up)
    return middle + reduced_precision_backward(matrix_product(activation, down_weight))

def reference(tokens, seq_lengths, attention_gain, query_weight, key_matrix, value_matrix, query_norm_gain, key_gain, out_weight, feed_gain, gate_weight, up_weight, down_weight, cotangent):
    weights = tuple((w.astype(jnp.float32) for w in (attention_gain, query_weight, key_matrix, value_matrix, query_norm_gain, key_gain, out_weight, feed_gain, gate_weight, up_weight, down_weight)))
    buffers = tokens.astype(jnp.float32).reshape(N_FSDP * N_REPLICA, TOK_DEV, MODEL_WIDTH)
    segment, position = jax.vmap(lambda row: layout(row, TOK_DEV))(seq_lengths)
    live = (segment > 0).astype(jnp.float32)
    grad_result = cotangent.astype(jnp.float32).reshape(buffers.shape) * live[..., None]
    block_layer = jax.checkpoint(layer)

    def forward(inputs, params):
        return lax.map(lambda item: block_layer(item[0], item[1], item[2], params), (inputs, segment, position))
    result, pullback = jax.vjp(forward, buffers, weights)
    grad_inputs, grad_params = pullback(grad_result)
    factor = 1.0 / math.sqrt(TOKENS)
    scaled = tuple((g * factor for g in grad_params))
    return (result.reshape(TOKENS, MODEL_WIDTH).astype(jnp.bfloat16), grad_inputs.reshape(TOKENS, MODEL_WIDTH).astype(jnp.bfloat16), scaled[0], scaled[1], scaled[2], scaled[3], scaled[4], scaled[5], scaled[6], scaled[7], scaled[8], scaled[9], scaled[10])
```

```python
import math

import jax
import jax.numpy as jnp
from jax import lax
from jax.sharding import PartitionSpec as P

QUERY_HEADS = 16
KEY_VALUE_HEADS = 8
HEAD_SIZE = 128
BLOCK = 128


norm_eps = 1e-06
rope_base = 1000000.0


def layout(lengths_row, token_count):
    blocks = (lengths_row + BLOCK - 1) // BLOCK
    ends = jnp.cumsum(blocks) * BLOCK
    starts = ends - blocks * BLOCK
    places = jnp.arange(token_count, dtype=jnp.int32)
    inside = (places[:, None] >= starts[None, :]) & (
        places[:, None] < starts[None, :] + lengths_row[None, :]
    )
    numbers = jnp.arange(lengths_row.shape[0], dtype=jnp.int32) + 1
    segment = jnp.sum(jnp.where(inside, numbers[None, :], 0), axis=1)
    position = jnp.sum(jnp.where(inside, places[:, None] - starts[None, :], 0), axis=1)
    return (segment, position)


def rope_tables(position):
    half = HEAD_SIZE // 2
    freq = jnp.exp(-math.log(rope_base) * 2.0 * jnp.arange(half, dtype=jnp.float32) / HEAD_SIZE)
    angle = position.astype(jnp.float32)[:, None] * freq[None, :]
    return (jnp.cos(angle)[:, None, :], jnp.sin(angle)[:, None, :])


def apply_rotary(value_rows, cosine_table, sine_table):
    half = HEAD_SIZE // 2
    first_half = value_rows[..., :half]
    second_half = value_rows[..., half:]
    return jnp.concatenate(
        [
            first_half * cosine_table - second_half * sine_table,
            second_half * cosine_table + first_half * sine_table,
        ],
        axis=-1,
    )


def unit_scale(value_rows):
    inverse = lax.rsqrt(jnp.mean(value_rows * value_rows, axis=-1, keepdims=True) + norm_eps)
    return (value_rows * inverse, inverse)


def norm_back(grad, unit, inverse, gain):
    scaled = grad * gain
    return inverse * (scaled - unit * jnp.mean(scaled * unit, axis=-1, keepdims=True))


def contract_rows(left, right):
    return lax.dot_general(
        left, right, (((0,), (0,)), ((), ())), preferred_element_type=jnp.float32
    )


def product_with_transpose(left, right):
    return lax.dot_general(
        left, right, (((1,), (1,)), ((), ())), preferred_element_type=jnp.float32
    )


def masked_scores(query_rows, key_rows, seg_rows, seg_keys, first):
    scores = jnp.einsum(
        "qgrd,kgd->grqk", query_rows, key_rows, preferred_element_type=jnp.float32
    ) / math.sqrt(HEAD_SIZE)
    rows_at = first + jnp.arange(query_rows.shape[0], dtype=jnp.int32)
    cols_at = jnp.arange(key_rows.shape[0], dtype=jnp.int32)
    allowed = (seg_rows[:, None] == seg_keys[None, :]) & (cols_at[None, :] <= rows_at[:, None])
    return jnp.where(allowed[None, None], scores, -1e30)


def local(
    tokens,
    seq_lengths,
    attention_gain,
    query_weight,
    key_matrix,
    value_matrix,
    query_norm_gain,
    key_gain,
    out_weight,
    feed_gain,
    gate_weight,
    up_weight,
    down_weight,
    cotangent,
):
    token_count = tokens.shape[0]
    head_groups = QUERY_HEADS // KEY_VALUE_HEADS
    rows_block = min(256, token_count)
    blocks = token_count // rows_block
    segment, position = layout(seq_lengths[0], token_count)
    cosine_table, sine_table = rope_tables(position)
    attention_set = (
        lax.all_gather(attention_gain, "fsdp", axis=0, tiled=True),
        lax.all_gather(query_weight, "fsdp", axis=0, tiled=True),
        lax.all_gather(key_matrix, "fsdp", axis=0, tiled=True),
        lax.all_gather(value_matrix, "fsdp", axis=0, tiled=True),
        lax.all_gather(query_norm_gain, "fsdp", axis=0, tiled=True),
        lax.all_gather(key_gain, "fsdp", axis=0, tiled=True),
        lax.all_gather(out_weight, "fsdp", axis=0, tiled=True),
    )
    first_gain, query_full, key_complete, value_full, query_scale, key_scale, out_full = (
        attention_set
    )
    first_gain = first_gain.astype(jnp.float32)
    query_scale = query_scale.astype(jnp.float32)
    key_scale = key_scale.astype(jnp.float32)
    inputs = tokens.astype(jnp.float32)
    unit_first, inverse_first = unit_scale(inputs)
    hidden_state = (unit_first * first_gain).astype(jnp.bfloat16)
    query_raw = jnp.dot(hidden_state, query_full, preferred_element_type=jnp.float32).reshape(
        token_count, QUERY_HEADS, HEAD_SIZE
    )
    key_unnormed = jnp.dot(hidden_state, key_complete, preferred_element_type=jnp.float32).reshape(
        token_count, KEY_VALUE_HEADS, HEAD_SIZE
    )
    value_reduced = jnp.dot(hidden_state, value_full, preferred_element_type=jnp.float32).astype(
        jnp.bfloat16
    )
    value_reduced = value_reduced.reshape(token_count, KEY_VALUE_HEADS, HEAD_SIZE)
    query_unit, query_inverse = unit_scale(query_raw)
    key_unit, key_inverse = unit_scale(key_unnormed)
    query_low = (
        apply_rotary(query_unit * query_scale, cosine_table, sine_table)
        .astype(jnp.bfloat16)
        .reshape(token_count, KEY_VALUE_HEADS, head_groups, HEAD_SIZE)
    )
    key_low = apply_rotary(key_unit * key_scale, cosine_table, sine_table).astype(jnp.bfloat16)
    block_outs = []
    tops = []
    totals = []
    for number in range(blocks):
        start = number * rows_block
        finish = start + rows_block
        scores = masked_scores(
            query_low[start:finish],
            key_low[:finish],
            segment[start:finish],
            segment[:finish],
            start,
        )
        top = jnp.max(scores, axis=-1, keepdims=True)
        weight = jnp.exp(scores - top)
        total = jnp.sum(weight, axis=-1, keepdims=True)
        probs_low = (weight / total).astype(jnp.bfloat16)
        block_outs.append(
            jnp.einsum(
                "grqk,kgd->qgrd",
                probs_low,
                value_reduced[:finish],
                preferred_element_type=jnp.float32,
            )
        )
        tops.append(top)
        totals.append(total)
    mixed_low = (
        jnp.concatenate(block_outs, axis=0)
        .reshape(token_count, QUERY_HEADS * HEAD_SIZE)
        .astype(jnp.bfloat16)
    )
    middle = inputs + jnp.dot(mixed_low, out_full, preferred_element_type=jnp.float32)
    feed_set = (
        lax.all_gather(feed_gain, "fsdp", axis=0, tiled=True),
        lax.all_gather(gate_weight, "fsdp", axis=0, tiled=True),
        lax.all_gather(up_weight, "fsdp", axis=0, tiled=True),
        lax.all_gather(down_weight, "fsdp", axis=0, tiled=True),
    )
    second_gain, gate_full, up_full, down_full = feed_set
    second_gain = second_gain.astype(jnp.float32)
    unit_second, inverse_second = unit_scale(middle)
    hidden_second = (unit_second * second_gain).astype(jnp.bfloat16)
    gate = jnp.dot(hidden_second, gate_full, preferred_element_type=jnp.float32)
    up_value = jnp.dot(hidden_second, up_full, preferred_element_type=jnp.float32)
    sigma = jax.nn.sigmoid(gate)
    silu_value = gate * sigma
    activation_low = (silu_value * up_value).astype(jnp.bfloat16)
    result = middle + jnp.dot(activation_low, down_full, preferred_element_type=jnp.float32)
    output = result.astype(jnp.bfloat16)
    live = (segment > 0).astype(jnp.float32)
    grad_result = cotangent.astype(jnp.float32) * live[:, None]
    feed_back = (
        lax.all_gather(feed_gain, "fsdp", axis=0, tiled=True),
        lax.all_gather(gate_weight, "fsdp", axis=0, tiled=True),
        lax.all_gather(up_weight, "fsdp", axis=0, tiled=True),
        lax.all_gather(down_weight, "fsdp", axis=0, tiled=True),
    )
    gate_back, up_back, down_back = (feed_back[1], feed_back[2], feed_back[3])
    grad_result_low = grad_result.astype(jnp.bfloat16)
    grad_down = contract_rows(activation_low, grad_result_low)
    grad_act = product_with_transpose(grad_result_low, down_back)
    grad_silu = grad_act * up_value
    gate_grad_low = (grad_silu * (sigma + gate * sigma * (1.0 - sigma))).astype(jnp.bfloat16)
    up_grad_low = (grad_act * silu_value).astype(jnp.bfloat16)
    grad_gate = contract_rows(hidden_second, gate_grad_low)
    grad_up = contract_rows(hidden_second, up_grad_low)
    grad_hidden_second = product_with_transpose(gate_grad_low, gate_back) + product_with_transpose(
        up_grad_low, up_back
    )
    grad_second_gain = jnp.sum(grad_hidden_second * unit_second, axis=0)
    grad_middle = grad_result + norm_back(
        grad_hidden_second, unit_second, inverse_second, second_gain
    )
    feed_shares = (
        lax.psum_scatter(
            grad_second_gain.astype(jnp.bfloat16), "fsdp", scatter_dimension=0, tiled=True
        ),
        lax.psum_scatter(
            grad_gate.astype(jnp.bfloat16), "fsdp", scatter_dimension=0, tiled=True
        ),
        lax.psum_scatter(
            grad_up.astype(jnp.bfloat16), "fsdp", scatter_dimension=0, tiled=True
        ),
        lax.psum_scatter(
            grad_down.astype(jnp.bfloat16), "fsdp", scatter_dimension=0, tiled=True
        ),
    )
    attention_back = (
        lax.all_gather(attention_gain, "fsdp", axis=0, tiled=True),
        lax.all_gather(query_weight, "fsdp", axis=0, tiled=True),
        lax.all_gather(key_matrix, "fsdp", axis=0, tiled=True),
        lax.all_gather(value_matrix, "fsdp", axis=0, tiled=True),
        lax.all_gather(query_norm_gain, "fsdp", axis=0, tiled=True),
        lax.all_gather(key_gain, "fsdp", axis=0, tiled=True),
        lax.all_gather(out_weight, "fsdp", axis=0, tiled=True),
    )
    query_back, key_back, value_back, output_backward = (
        attention_back[1],
        attention_back[2],
        attention_back[3],
        attention_back[6],
    )
    middle_reduced = grad_middle.astype(jnp.bfloat16)
    grad_out = contract_rows(mixed_low, middle_reduced)
    grad_mixed_low = (
        product_with_transpose(middle_reduced, output_backward)
        .astype(jnp.bfloat16)
        .reshape(token_count, KEY_VALUE_HEADS, head_groups, HEAD_SIZE)
    )
    key_gradient_total = jnp.zeros((token_count, KEY_VALUE_HEADS, HEAD_SIZE), jnp.float32)
    value_gradient_total = jnp.zeros((token_count, KEY_VALUE_HEADS, HEAD_SIZE), jnp.float32)
    query_grads = []
    for number in range(blocks):
        start = number * rows_block
        finish = start + rows_block
        scores = masked_scores(
            query_low[start:finish],
            key_low[:finish],
            segment[start:finish],
            segment[:finish],
            start,
        )
        probs = jnp.exp(scores - tops[number]) / totals[number]
        probs_low = probs.astype(jnp.bfloat16)
        grad_slice = grad_mixed_low[start:finish]
        value_gradient_total = value_gradient_total.at[:finish].add(
            jnp.einsum("grqk,qgrd->kgd", probs_low, grad_slice, preferred_element_type=jnp.float32)
        )
        grad_probs = jnp.einsum(
            "qgrd,kgd->grqk", grad_slice, value_reduced[:finish], preferred_element_type=jnp.float32
        )
        grad_scores = probs * (grad_probs - jnp.sum(probs * grad_probs, axis=-1, keepdims=True))
        scores_low = grad_scores.astype(jnp.bfloat16)
        query_grads.append(
            jnp.einsum(
                "grqk,kgd->qgrd", scores_low, key_low[:finish], preferred_element_type=jnp.float32
            )
            / math.sqrt(HEAD_SIZE)
        )
        key_gradient_total = key_gradient_total.at[:finish].add(
            jnp.einsum(
                "grqk,qgrd->kgd",
                scores_low,
                query_low[start:finish],
                preferred_element_type=jnp.float32,
            )
            / math.sqrt(HEAD_SIZE)
        )
    grad_query_rot = jnp.concatenate(query_grads, axis=0).reshape(
        token_count, QUERY_HEADS, HEAD_SIZE
    )
    grad_query_norm = apply_rotary(grad_query_rot, cosine_table, -sine_table)
    grad_query_scale = jnp.sum(grad_query_norm * query_unit, axis=(0, 1))
    query_grad_low = norm_back(grad_query_norm, query_unit, query_inverse, query_scale)
    query_grad_low = query_grad_low.astype(jnp.bfloat16).reshape(
        token_count, QUERY_HEADS * HEAD_SIZE
    )
    grad_key_norm = apply_rotary(key_gradient_total, cosine_table, -sine_table)
    grad_key_scale = jnp.sum(grad_key_norm * key_unit, axis=(0, 1))
    key_gradient_reduced = norm_back(grad_key_norm, key_unit, key_inverse, key_scale)
    key_gradient_reduced = key_gradient_reduced.astype(jnp.bfloat16).reshape(
        token_count, KEY_VALUE_HEADS * HEAD_SIZE
    )
    value_gradient_reduced = value_gradient_total.astype(jnp.bfloat16).reshape(
        token_count, KEY_VALUE_HEADS * HEAD_SIZE
    )
    grad_query = contract_rows(hidden_state, query_grad_low)
    grad_key = contract_rows(hidden_state, key_gradient_reduced)
    grad_value = contract_rows(hidden_state, value_gradient_reduced)
    grad_hidden = (
        product_with_transpose(query_grad_low, query_back)
        + product_with_transpose(key_gradient_reduced, key_back)
        + product_with_transpose(value_gradient_reduced, value_back)
    )
    grad_first_gain = jnp.sum(grad_hidden * unit_first, axis=0)
    grad_inputs = grad_middle + norm_back(grad_hidden, unit_first, inverse_first, first_gain)
    attention_shares = (
        lax.psum_scatter(
            grad_first_gain.astype(jnp.bfloat16), "fsdp", scatter_dimension=0, tiled=True
        ),
        lax.psum_scatter(
            grad_query.astype(jnp.bfloat16), "fsdp", scatter_dimension=0, tiled=True
        ),
        lax.psum_scatter(
            grad_key.astype(jnp.bfloat16), "fsdp", scatter_dimension=0, tiled=True
        ),
        lax.psum_scatter(
            grad_value.astype(jnp.bfloat16), "fsdp", scatter_dimension=0, tiled=True
        ),
        lax.psum_scatter(
            grad_query_scale.astype(jnp.bfloat16), "fsdp", scatter_dimension=0, tiled=True
        ),
        lax.psum_scatter(
            grad_key_scale.astype(jnp.bfloat16), "fsdp", scatter_dimension=0, tiled=True
        ),
        lax.psum_scatter(
            grad_out.astype(jnp.bfloat16), "fsdp", scatter_dimension=0, tiled=True
        ),
    )
    summed = lax.psum(
        (
            attention_shares[0],
            attention_shares[1],
            attention_shares[2],
            attention_shares[3],
            attention_shares[4],
            attention_shares[5],
            attention_shares[6],
            feed_shares[0],
            feed_shares[1],
            feed_shares[2],
            feed_shares[3],
        ),
        "replica",
    )
    summed = tuple(share.astype(jnp.float32) for share in summed)
    attention_shares = summed[:7]
    feed_shares = summed[7:]
    factor = 1.0 / math.sqrt(token_count * lax.axis_size("fsdp") * lax.axis_size("replica"))
    return (
        output,
        grad_inputs.astype(jnp.bfloat16),
        attention_shares[0] * factor,
        attention_shares[1] * factor,
        attention_shares[2] * factor,
        attention_shares[3] * factor,
        attention_shares[4] * factor,
        attention_shares[5] * factor,
        attention_shares[6] * factor,
        feed_shares[0] * factor,
        feed_shares[1] * factor,
        feed_shares[2] * factor,
        feed_shares[3] * factor,
    )


def solution(mesh):
    in_specs = (
        P(("fsdp", "replica"), None),
        P(("fsdp", "replica"), None),
        P("fsdp"),
        P("fsdp", None),
        P("fsdp", None),
        P("fsdp", None),
        P("fsdp"),
        P("fsdp"),
        P("fsdp", None),
        P("fsdp"),
        P("fsdp", None),
        P("fsdp", None),
        P("fsdp", None),
        P(("fsdp", "replica"), None),
    )
    out_specs = (
        P(("fsdp", "replica"), None),
        P(("fsdp", "replica"), None),
        P("fsdp"),
        P("fsdp", None),
        P("fsdp", None),
        P("fsdp", None),
        P("fsdp"),
        P("fsdp"),
        P("fsdp", None),
        P("fsdp"),
        P("fsdp", None),
        P("fsdp", None),
        P("fsdp", None),
    )
    return jax.shard_map(local, mesh=mesh, in_specs=in_specs, out_specs=out_specs, check_vma=False)
```

```python
import math

import jax
import jax.numpy as jnp
from jax import lax
from jax.sharding import PartitionSpec as P

QUERY_HEADS = 16
KEY_VALUE_HEADS = 8
HEAD_SIZE = 128
BLOCK = 128


norm_eps = 1e-06
rope_base = 1000000.0


def layout(lengths_row, token_count):
    blocks = (lengths_row + BLOCK - 1) // BLOCK
    ends = jnp.cumsum(blocks) * BLOCK
    starts = ends - blocks * BLOCK
    places = jnp.arange(token_count, dtype=jnp.int32)
    inside = (places[:, None] >= starts[None, :]) & (
        places[:, None] < starts[None, :] + lengths_row[None, :]
    )
    numbers = jnp.arange(lengths_row.shape[0], dtype=jnp.int32) + 1
    segment = jnp.sum(jnp.where(inside, numbers[None, :], 0), axis=1)
    position = jnp.sum(jnp.where(inside, places[:, None] - starts[None, :], 0), axis=1)
    return (segment, position)


def rope_tables(position):
    half = HEAD_SIZE // 2
    freq = jnp.exp(-math.log(rope_base) * 2.0 * jnp.arange(half, dtype=jnp.float32) / HEAD_SIZE)
    angle = position.astype(jnp.float32)[:, None] * freq[None, :]
    return (jnp.cos(angle)[:, None, :], jnp.sin(angle)[:, None, :])


def apply_rotary(value_rows, cosine_table, sine_table):
    half = HEAD_SIZE // 2
    first_half = value_rows[..., :half]
    second_half = value_rows[..., half:]
    return jnp.concatenate(
        [
            first_half * cosine_table - second_half * sine_table,
            second_half * cosine_table + first_half * sine_table,
        ],
        axis=-1,
    )


def unit_scale(value_rows):
    inverse = lax.rsqrt(jnp.mean(value_rows * value_rows, axis=-1, keepdims=True) + norm_eps)
    return (value_rows * inverse, inverse)


def norm_back(grad, unit, inverse, gain):
    scaled = grad * gain
    return inverse * (scaled - unit * jnp.mean(scaled * unit, axis=-1, keepdims=True))


def contract_rows(left, right):
    return lax.dot_general(
        left, right, (((0,), (0,)), ((), ())), preferred_element_type=jnp.float32
    )


def product_with_transpose(left, right):
    return lax.dot_general(
        left, right, (((1,), (1,)), ((), ())), preferred_element_type=jnp.float32
    )


def partner(bit):
    return [(i, i ^ bit) for i in range(lax.axis_size("fsdp"))]


def split_columns(left, core):
    rows, width = left.shape
    parts = left.reshape(rows, 2, 2, width // 4)
    here = lax.dynamic_index_in_dim(parts, core, 2, keepdims=False)
    there = lax.dynamic_index_in_dim(parts, 1 - core, 2, keepdims=False)
    return here.reshape(rows, width // 2), there.reshape(rows, width // 2)


def start_shares(left, right):
    core = lax.axis_index("fsdp") % 2
    here, there = split_columns(left, core)
    sent = contract_rows(there, right).astype(jnp.bfloat16)
    return here, right, sent


def chip_shares(started):
    here, right, sent = started
    received = lax.ppermute(sent, "fsdp", partner(1))
    return (contract_rows(here, right) + received.astype(jnp.float32)).astype(jnp.bfloat16)


def finish_shares(half):
    side = lax.axis_index("fsdp") // 2
    half = half.reshape(2, half.shape[0] // 2, half.shape[1])
    kept = lax.dynamic_index_in_dim(half, side, 0, keepdims=False)
    sent = lax.dynamic_index_in_dim(half, 1 - side, 0, keepdims=False)
    received = lax.ppermute(sent, "fsdp", partner(2))
    return (kept.astype(jnp.float32) + received.astype(jnp.float32)).astype(jnp.bfloat16)


def masked_scores(query_rows, key_rows, seg_rows, seg_keys, first):
    scores = jnp.einsum(
        "qgrd,kgd->grqk", query_rows, key_rows, preferred_element_type=jnp.float32
    ) / math.sqrt(HEAD_SIZE)
    rows_at = first + jnp.arange(query_rows.shape[0], dtype=jnp.int32)
    cols_at = jnp.arange(key_rows.shape[0], dtype=jnp.int32)
    allowed = (seg_rows[:, None] == seg_keys[None, :]) & (cols_at[None, :] <= rows_at[:, None])
    return jnp.where(allowed[None, None], scores, -1e30)


def local(
    tokens,
    seq_lengths,
    attention_gain,
    query_weight,
    key_matrix,
    value_matrix,
    query_norm_gain,
    key_gain,
    out_weight,
    feed_gain,
    gate_weight,
    up_weight,
    down_weight,
    cotangent,
):
    token_count = tokens.shape[0]
    head_groups = QUERY_HEADS // KEY_VALUE_HEADS
    rows_block = min(256, token_count)
    blocks = token_count // rows_block
    segment, position = layout(seq_lengths[0], token_count)
    cosine_table, sine_table = rope_tables(position)
    attention_set = (
        lax.all_gather(attention_gain, "fsdp", axis=0, tiled=True),
        lax.all_gather(query_weight, "fsdp", axis=0, tiled=True),
        lax.all_gather(key_matrix, "fsdp", axis=0, tiled=True),
        lax.all_gather(value_matrix, "fsdp", axis=0, tiled=True),
        lax.all_gather(query_norm_gain, "fsdp", axis=0, tiled=True),
        lax.all_gather(key_gain, "fsdp", axis=0, tiled=True),
        lax.all_gather(out_weight, "fsdp", axis=0, tiled=True),
    )
    first_gain, query_full, key_complete, value_full, query_scale, key_scale, out_full = (
        attention_set
    )
    first_gain = first_gain.astype(jnp.float32)
    query_scale = query_scale.astype(jnp.float32)
    key_scale = key_scale.astype(jnp.float32)
    inputs = tokens.astype(jnp.float32)
    unit_first, inverse_first = unit_scale(inputs)
    hidden_state = (unit_first * first_gain).astype(jnp.bfloat16)
    query_raw = jnp.dot(hidden_state, query_full, preferred_element_type=jnp.float32).reshape(
        token_count, QUERY_HEADS, HEAD_SIZE
    )
    key_unnormed = jnp.dot(hidden_state, key_complete, preferred_element_type=jnp.float32).reshape(
        token_count, KEY_VALUE_HEADS, HEAD_SIZE
    )
    value_reduced = jnp.dot(hidden_state, value_full, preferred_element_type=jnp.float32).astype(
        jnp.bfloat16
    )
    value_reduced = value_reduced.reshape(token_count, KEY_VALUE_HEADS, HEAD_SIZE)
    query_unit, query_inverse = unit_scale(query_raw)
    key_unit, key_inverse = unit_scale(key_unnormed)
    query_low = (
        apply_rotary(query_unit * query_scale, cosine_table, sine_table)
        .astype(jnp.bfloat16)
        .reshape(token_count, KEY_VALUE_HEADS, head_groups, HEAD_SIZE)
    )
    key_low = apply_rotary(key_unit * key_scale, cosine_table, sine_table).astype(jnp.bfloat16)
    block_outs = []
    tops = []
    totals = []
    for number in range(blocks):
        start = number * rows_block
        finish = start + rows_block
        scores = masked_scores(
            query_low[start:finish],
            key_low[:finish],
            segment[start:finish],
            segment[:finish],
            start,
        )
        top = jnp.max(scores, axis=-1, keepdims=True)
        weight = jnp.exp(scores - top)
        total = jnp.sum(weight, axis=-1, keepdims=True)
        probs_low = (weight / total).astype(jnp.bfloat16)
        block_outs.append(
            jnp.einsum(
                "grqk,kgd->qgrd",
                probs_low,
                value_reduced[:finish],
                preferred_element_type=jnp.float32,
            )
        )
        tops.append(top)
        totals.append(total)
    mixed_low = (
        jnp.concatenate(block_outs, axis=0)
        .reshape(token_count, QUERY_HEADS * HEAD_SIZE)
        .astype(jnp.bfloat16)
    )
    middle = inputs + jnp.dot(mixed_low, out_full, preferred_element_type=jnp.float32)
    feed_set = (
        lax.all_gather(feed_gain, "fsdp", axis=0, tiled=True),
        lax.all_gather(gate_weight, "fsdp", axis=0, tiled=True),
        lax.all_gather(up_weight, "fsdp", axis=0, tiled=True),
        lax.all_gather(down_weight, "fsdp", axis=0, tiled=True),
    )
    second_gain, gate_full, up_full, down_full = feed_set
    second_gain = second_gain.astype(jnp.float32)
    unit_second, inverse_second = unit_scale(middle)
    hidden_second = (unit_second * second_gain).astype(jnp.bfloat16)
    gate = jnp.dot(hidden_second, gate_full, preferred_element_type=jnp.float32)
    up_value = jnp.dot(hidden_second, up_full, preferred_element_type=jnp.float32)
    sigma = jax.nn.sigmoid(gate)
    silu_value = gate * sigma
    activation_low = (silu_value * up_value).astype(jnp.bfloat16)
    result = middle + jnp.dot(activation_low, down_full, preferred_element_type=jnp.float32)
    output = result.astype(jnp.bfloat16)
    live = (segment > 0).astype(jnp.float32)
    grad_result = cotangent.astype(jnp.float32) * live[:, None]
    feed_back = (
        lax.all_gather(feed_gain, "fsdp", axis=0, tiled=True),
        lax.all_gather(gate_weight, "fsdp", axis=0, tiled=True),
        lax.all_gather(up_weight, "fsdp", axis=0, tiled=True),
        lax.all_gather(down_weight, "fsdp", axis=0, tiled=True),
    )
    gate_back, up_back, down_back = (feed_back[1], feed_back[2], feed_back[3])
    grad_result_low = grad_result.astype(jnp.bfloat16)
    grad_down = start_shares(activation_low, grad_result_low)
    grad_act = product_with_transpose(grad_result_low, down_back)
    grad_silu = grad_act * up_value
    gate_grad_low = (grad_silu * (sigma + gate * sigma * (1.0 - sigma))).astype(jnp.bfloat16)
    up_grad_low = (grad_act * silu_value).astype(jnp.bfloat16)
    grad_gate = start_shares(hidden_second, gate_grad_low)
    grad_up = start_shares(hidden_second, up_grad_low)
    grad_hidden_second = product_with_transpose(gate_grad_low, gate_back) + product_with_transpose(
        up_grad_low, up_back
    )
    grad_second_gain = jnp.sum(grad_hidden_second * unit_second, axis=0)
    grad_middle = grad_result + norm_back(
        grad_hidden_second, unit_second, inverse_second, second_gain
    )
    attention_back = (
        lax.all_gather(attention_gain, "fsdp", axis=0, tiled=True),
        lax.all_gather(query_weight, "fsdp", axis=0, tiled=True),
        lax.all_gather(key_matrix, "fsdp", axis=0, tiled=True),
        lax.all_gather(value_matrix, "fsdp", axis=0, tiled=True),
        lax.all_gather(query_norm_gain, "fsdp", axis=0, tiled=True),
        lax.all_gather(key_gain, "fsdp", axis=0, tiled=True),
        lax.all_gather(out_weight, "fsdp", axis=0, tiled=True),
    )
    query_back, key_back, value_back, output_backward = (
        attention_back[1],
        attention_back[2],
        attention_back[3],
        attention_back[6],
    )
    middle_reduced = grad_middle.astype(jnp.bfloat16)
    middle_reduced, grad_down, grad_gate, grad_up = lax.optimization_barrier(
        (middle_reduced, grad_down, grad_gate, grad_up)
    )
    grad_out = start_shares(mixed_low, middle_reduced)
    grad_mixed_low = (
        product_with_transpose(middle_reduced, output_backward)
        .astype(jnp.bfloat16)
        .reshape(token_count, KEY_VALUE_HEADS, head_groups, HEAD_SIZE)
    )
    key_gradient_total = jnp.zeros((token_count, KEY_VALUE_HEADS, HEAD_SIZE), jnp.float32)
    value_gradient_total = jnp.zeros((token_count, KEY_VALUE_HEADS, HEAD_SIZE), jnp.float32)
    query_grads = []
    for number in range(blocks):
        start = number * rows_block
        finish = start + rows_block
        scores = masked_scores(
            query_low[start:finish],
            key_low[:finish],
            segment[start:finish],
            segment[:finish],
            start,
        )
        probs = jnp.exp(scores - tops[number]) / totals[number]
        probs_low = probs.astype(jnp.bfloat16)
        grad_slice = grad_mixed_low[start:finish]
        value_gradient_total = value_gradient_total.at[:finish].add(
            jnp.einsum("grqk,qgrd->kgd", probs_low, grad_slice, preferred_element_type=jnp.float32)
        )
        grad_probs = jnp.einsum(
            "qgrd,kgd->grqk", grad_slice, value_reduced[:finish], preferred_element_type=jnp.float32
        )
        grad_scores = probs * (grad_probs - jnp.sum(probs * grad_probs, axis=-1, keepdims=True))
        scores_low = grad_scores.astype(jnp.bfloat16)
        query_grads.append(
            jnp.einsum(
                "grqk,kgd->qgrd", scores_low, key_low[:finish], preferred_element_type=jnp.float32
            )
            / math.sqrt(HEAD_SIZE)
        )
        key_gradient_total = key_gradient_total.at[:finish].add(
            jnp.einsum(
                "grqk,qgrd->kgd",
                scores_low,
                query_low[start:finish],
                preferred_element_type=jnp.float32,
            )
            / math.sqrt(HEAD_SIZE)
        )
    query_grads, key_gradient_total, value_gradient_total, feed_halves = lax.optimization_barrier(
        (
            query_grads,
            key_gradient_total,
            value_gradient_total,
            (chip_shares(grad_gate), chip_shares(grad_up), chip_shares(grad_down)),
        )
    )
    feed_summed = lax.psum(tuple(finish_shares(half) for half in feed_halves), "replica")
    grad_query_rot = jnp.concatenate(query_grads, axis=0).reshape(
        token_count, QUERY_HEADS, HEAD_SIZE
    )
    grad_query_norm = apply_rotary(grad_query_rot, cosine_table, -sine_table)
    grad_query_scale = jnp.sum(grad_query_norm * query_unit, axis=(0, 1))
    query_grad_low = norm_back(grad_query_norm, query_unit, query_inverse, query_scale)
    query_grad_low = query_grad_low.astype(jnp.bfloat16).reshape(
        token_count, QUERY_HEADS * HEAD_SIZE
    )
    grad_key_norm = apply_rotary(key_gradient_total, cosine_table, -sine_table)
    grad_key_scale = jnp.sum(grad_key_norm * key_unit, axis=(0, 1))
    key_gradient_reduced = norm_back(grad_key_norm, key_unit, key_inverse, key_scale)
    key_gradient_reduced = key_gradient_reduced.astype(jnp.bfloat16).reshape(
        token_count, KEY_VALUE_HEADS * HEAD_SIZE
    )
    value_gradient_reduced = value_gradient_total.astype(jnp.bfloat16).reshape(
        token_count, KEY_VALUE_HEADS * HEAD_SIZE
    )
    grad_value = start_shares(hidden_state, value_gradient_reduced)
    grad_query = start_shares(hidden_state, query_grad_low)
    grad_key = start_shares(hidden_state, key_gradient_reduced)
    grad_hidden = (
        product_with_transpose(query_grad_low, query_back)
        + product_with_transpose(key_gradient_reduced, key_back)
        + product_with_transpose(value_gradient_reduced, value_back)
    )
    grad_first_gain = jnp.sum(grad_hidden * unit_first, axis=0)
    grad_inputs = grad_middle + norm_back(grad_hidden, unit_first, inverse_first, first_gain)
    attention_shares = (
        finish_shares(chip_shares(grad_query)),
        finish_shares(chip_shares(grad_key)),
        finish_shares(chip_shares(grad_value)),
        finish_shares(chip_shares(grad_out)),
    )
    attention_shares, feed_summed = lax.optimization_barrier((attention_shares, feed_summed))
    attention_summed = lax.psum(attention_shares, "replica")
    gains = lax.psum(
        jnp.concatenate([grad_first_gain, grad_second_gain, grad_query_scale, grad_key_scale]),
        ("fsdp", "replica"),
    )
    place = lax.axis_index("fsdp")
    groups = lax.axis_size("fsdp")
    gain_shares = []
    begin = 0
    for grad in (grad_first_gain, grad_second_gain, grad_query_scale, grad_key_scale):
        length = grad.shape[0] // groups
        gain_shares.append(lax.dynamic_slice(gains, (begin + place * length,), (length,)))
        begin += grad.shape[0]
    first_share, second_share, query_share, key_share = gain_shares
    wide = [share.astype(jnp.float32) for share in attention_summed + feed_summed]
    factor = 1.0 / math.sqrt(token_count * lax.axis_size("fsdp") * lax.axis_size("replica"))
    return (
        output,
        grad_inputs.astype(jnp.bfloat16),
        first_share * factor,
        wide[0] * factor,
        wide[1] * factor,
        wide[2] * factor,
        query_share * factor,
        key_share * factor,
        wide[3] * factor,
        second_share * factor,
        wide[4] * factor,
        wide[5] * factor,
        wide[6] * factor,
    )


def solution(mesh):
    in_specs = (
        P(("fsdp", "replica"), None),
        P(("fsdp", "replica"), None),
        P("fsdp"),
        P("fsdp", None),
        P("fsdp", None),
        P("fsdp", None),
        P("fsdp"),
        P("fsdp"),
        P("fsdp", None),
        P("fsdp"),
        P("fsdp", None),
        P("fsdp", None),
        P("fsdp", None),
        P(("fsdp", "replica"), None),
    )
    out_specs = (
        P(("fsdp", "replica"), None),
        P(("fsdp", "replica"), None),
        P("fsdp"),
        P("fsdp", None),
        P("fsdp", None),
        P("fsdp", None),
        P("fsdp"),
        P("fsdp"),
        P("fsdp", None),
        P("fsdp"),
        P("fsdp", None),
        P("fsdp", None),
        P("fsdp", None),
    )
    return jax.shard_map(local, mesh=mesh, in_specs=in_specs, out_specs=out_specs, check_vma=False)
```
